256 devices in a mesh: gz: 32 (over x, z), rows: 8 (over y, core).
Axes of the slice: x: 4, y: 4, z: 8, core: 2. Of those that a mesh axis runs over, the one named last changes fastest.
Arguments:
- sections: bfloat16 [32, 2048, 4096], P('gz', 'rows'), may hold values from -4 to 4
- peaks: int32 [32, 2, 2, 4], P('gz'), may hold values from -16 to 16, as said below
Outputs:
- field: float32 [32, 2, 2048, 4096], P('gz', None, 'rows')
- pair_offsets: float32 [32, 2, 2, 4], P('gz')
- residual: bfloat16 [32, 2048, 4096], P('gz', 'rows')
The draws below stay inside these ranges and needn't reach their ends.
Inputs may be any that keep to these rules, and one draw needn't show every extreme that they name: `peaks`: in every draw the first section's first patch has row offset 16 and column offset -16.
All inputs are finite; a program needn't handle non-finite values.
Results may differ from the reference program's by a relative error of at most 0.001.
Values may be sent and summed in bfloat16 or wider, within the bound.
No kernel may reach another device: no remote copies, remote signals or barrier semaphores. Data moves between devices by JAX's collectives and lax.ppermute only.
A program may use at most 64 MiB of HBM per device.

```python
import jax
import jax.numpy as jnp
import numpy as np
from jax import lax

W = 4096
PATCH = 1024
MAXOFF = 16
H = 2048
SECTIONS = 32
PGY = 2
PGX = 4


def joint_shifts(key):
    peaks = jax.random.randint(jax.random.fold_in(key, 11), (SECTIONS, 2, PGY, PGX), -MAXOFF, MAXOFF + 1)
    peaks = peaks.at[0, 0, 0, 0].set(MAXOFF).at[0, 1, 0, 0].set(-MAXOFF)
    fraction = jax.random.uniform(jax.random.fold_in(key, 12), (SECTIONS, 2, PGY, PGX), minval=-0.5, maxval=0.5)
    total = jnp.cumsum(peaks.astype(jnp.float32) + fraction, axis=0)
    return (peaks, total)


def draw_peaks(key, part):
    return joint_shifts(key)[0]


def draw_sections(key, part):
    _, total = joint_shifts(key)
    waves = 12
    wave_key = jax.random.fold_in(key, 13)
    length = jnp.exp(jax.random.uniform(jax.random.fold_in(wave_key, 1), (waves,), minval=jnp.log(12.0), maxval=jnp.log(64.0)))
    heading = jax.random.uniform(jax.random.fold_in(wave_key, 2), (waves,), minval=-3.14159, maxval=3.14159)
    phase = jax.random.uniform(jax.random.fold_in(wave_key, 3), (waves,), minval=-3.14159, maxval=3.14159)
    amplitude = 0.25 * jnp.ones((waves,), jnp.float32)
    noise_scale = 0.05
    freq_y = 6.2831853 / length * jnp.sin(heading)
    freq_x = 6.2831853 / length * jnp.cos(heading)
    row_index = jnp.arange(H)
    col_index = jnp.arange(W)
    patch_y = row_index // PATCH
    patch_x = col_index // PATCH
    noise_key = jax.random.fold_in(key, 14)

    def single(index):
        shift_y = total[index, 0][patch_y][:, patch_x]
        shift_x = total[index, 1][patch_y][:, patch_x]
        coord_y = row_index.astype(jnp.float32)[:, None] + shift_y
        coord_x = col_index.astype(jnp.float32)[None, :] + shift_x
        image = jnp.zeros((H, W), jnp.float32)
        for wave in range(waves):
            image = image + amplitude[wave] * jnp.cos(freq_y[wave] * coord_y + freq_x[wave] * coord_x + phase[wave])
        noise = jax.random.normal(jax.random.fold_in(noise_key, index), (H, W)) * noise_scale
        return jnp.clip(image + noise, -4.0, 4.0)
    return lax.map(single, jnp.arange(SECTIONS)).astype(jnp.bfloat16)


def setup_inputs(seed: int = 0) -> dict:
    streams_of = jax.random.split(jax.random.key(seed), 3)
    sections = draw_sections(jax.random.fold_in(streams_of[2], 71), 0)
    peaks = draw_peaks(jax.random.fold_in(streams_of[2], 71), 0)
    return dict(sections=sections, peaks=peaks)


LAMBDA = 0.002
RIDGE = 0.05


def invert_three(matrix):
    a, b, c = matrix[0, 0], matrix[0, 1], matrix[0, 2]
    d, e, f = matrix[1, 0], matrix[1, 1], matrix[1, 2]
    g, h, k = matrix[2, 0], matrix[2, 1], matrix[2, 2]
    cof = np.array([[e * k - f * h, c * h - b * k, b * f - c * e],
                    [f * g - d * k, a * k - c * g, c * d - a * f],
                    [d * h - e * g, b * g - a * h, a * e - b * d]])
    return cof / (a * (e * k - f * h) - b * (d * k - f * g) + c * (d * h - e * g))


def fit_table(pgy, pgx, patch, height, width):
    yy = ((np.arange(pgy) + 0.5) * patch - height / 2.0) / height
    xx = ((np.arange(pgx) + 0.5) * patch - width / 2.0) / width
    design = np.stack([np.repeat(yy, pgx), np.tile(xx, pgy), np.ones(pgy * pgx)], 1)
    ridge_matrix = np.array([[RIDGE, 0.0, 0.0], [0.0, RIDGE, 0.0], [0.0, 0.0, 0.0]])
    gram = design.T @ design + ridge_matrix
    return invert_three(gram) @ design.T


def spread(count, patch, nodes, start):
    pos = (start + jnp.arange(count).astype(jnp.float32) + 0.5) / patch - 0.5
    pos = jnp.clip(pos, 0.0, nodes - 1.0)
    return jnp.maximum(0.0, 1.0 - jnp.abs(pos[:, None] - jnp.arange(nodes).astype(jnp.float32)[None, :]))


def moments(current, window):
    centre = window[1:-1, 1:-1]
    grad_y = (window[2:, 1:-1] - window[:-2, 1:-1]) * 0.5
    grad_x = (window[1:-1, 2:] - window[1:-1, :-2]) * 0.5
    error = current - centre
    sums = jnp.stack([jnp.sum(grad_y * grad_y), jnp.sum(grad_y * grad_x), jnp.sum(grad_x * grad_x),
                      jnp.sum(grad_y * error), jnp.sum(grad_x * error)])
    return sums, error


def solve_pairs(sums, peak_grid):
    damping = LAMBDA * PATCH * PATCH
    first = sums[0] + damping
    cross = sums[1]
    second = sums[2] + damping
    determinant = first * second - cross * cross
    step_y = (second * sums[3] - cross * sums[4]) / determinant
    step_x = (first * sums[4] - cross * sums[3]) / determinant
    return peak_grid.astype(jnp.float32) + jnp.stack([step_y, step_x])


def transform(offsets, table, height, width):
    flat = offsets.reshape(2, -1)
    coef = jnp.dot(flat, table.T, precision=lax.Precision.HIGHEST)
    return jnp.eye(2, dtype=jnp.float32) + jnp.stack([coef[:, 0] / height, coef[:, 1] / width], axis=1)


def reference(sections, peaks):
    count, height, width = sections.shape
    pgy = height // PATCH
    pgx = width // PATCH
    margin = MAXOFF + 1
    table = jnp.asarray(fit_table(pgy, pgx, PATCH, height, width), jnp.float32)

    def pair(index):
        current = sections[index].astype(jnp.float32)
        before = jnp.where(index > 0, sections[jnp.maximum(index - 1, 0)].astype(jnp.float32), 0.0)
        padded = jnp.pad(before, margin)
        grid = peaks[index]
        rows_out = []
        errors_rows = []
        for i in range(pgy):
            cols_out = []
            errors_cols = []
            for j in range(pgx):
                start_y = (i * PATCH + margin - 1 + grid[0, i, j]).astype(jnp.int32)
                start_x = (j * PATCH + margin - 1 + grid[1, i, j]).astype(jnp.int32)
                window = lax.dynamic_slice(padded, (start_y, start_x), (PATCH + 2, PATCH + 2))
                piece = current[i * PATCH:(i + 1) * PATCH, j * PATCH:(j + 1) * PATCH]
                sums, error = moments(piece, window)
                cols_out.append(sums)
                errors_cols.append(error)
            rows_out.append(jnp.stack(cols_out, axis=1))
            errors_rows.append(jnp.concatenate(errors_cols, axis=1))
        sums = jnp.stack(rows_out, axis=1)
        image = jnp.concatenate(errors_rows, axis=0).astype(jnp.bfloat16)
        return solve_pairs(sums, grid), image

    offsets, residual = lax.map(pair, jnp.arange(count))

    def advance(carry, item):
        linear = transform(item, table, height, width)
        moved = jnp.dot(linear, carry, precision=lax.Precision.HIGHEST) + item.reshape(2, -1)
        return moved, moved

    _, cumulative = lax.scan(advance, jnp.zeros((2, pgy * pgx), jnp.float32), offsets)
    along_rows = spread(height, PATCH, pgy, 0)
    along_cols = spread(width, PATCH, pgx, 0)

    def dense(nodes):
        grid = nodes.reshape(2, pgy, pgx)
        wide = jnp.einsum('kij,cj->kic', grid, along_cols, precision=lax.Precision.HIGHEST)
        return jnp.einsum('ri,kic->krc', along_rows, wide, precision=lax.Precision.HIGHEST)

    field = lax.map(dense, cumulative)
    return field, offsets, residual
```

```python
import jax
import jax.numpy as jnp
import numpy as np
from jax import lax
from jax.experimental import pallas as pl
from jax.experimental.pallas import tpu as pltpu
from jax.sharding import PartitionSpec as P

PATCH = 1024
LAMBDA = 0.002
RIDGE = 0.05

PGY = 2
PGX = 4
HALF = PGX // 2
SPLIT = HALF * PATCH
LANES = 128
BLOCK = 256
EDGE = 32
EXTRA = 16
MIDDLES = (192,)
TAILS = (112, 112, 96)
ROWS_CHUNK = 32
F32 = jnp.float32
BF16 = jnp.bfloat16


def shift(value, axis, steps):
    count = lax.axis_size(axis)
    first, last = (max(0, -steps), min(count, count - steps))
    return lax.ppermute(value, axis, [(source, source + steps) for source in range(first, last)])


def invert_three(matrix):
    a, b, c = (matrix[0, 0], matrix[0, 1], matrix[0, 2])
    d, e, f = (matrix[1, 0], matrix[1, 1], matrix[1, 2])
    g, h, k = (matrix[2, 0], matrix[2, 1], matrix[2, 2])
    cof = np.array(
        [
            [e * k - f * h, c * h - b * k, b * f - c * e],
            [f * g - d * k, a * k - c * g, c * d - a * f],
            [d * h - e * g, b * g - a * h, a * e - b * d],
        ]
    )
    return cof / (a * (e * k - f * h) - b * (d * k - f * g) + c * (d * h - e * g))


def fit_table(pgy, pgx, patch, height, width):
    yy = ((np.arange(pgy) + 0.5) * patch - height / 2.0) / height
    xx = ((np.arange(pgx) + 0.5) * patch - width / 2.0) / width
    design = np.stack([np.repeat(yy, pgx), np.tile(xx, pgy), np.ones(pgy * pgx)], 1)
    ridge_matrix = np.array([[RIDGE, 0.0, 0.0], [0.0, RIDGE, 0.0], [0.0, 0.0, 0.0]])
    gram = design.T @ design + ridge_matrix
    return invert_three(gram) @ design.T


def shift_matrices(b):
    d = (
        lax.broadcasted_iota(jnp.int32, (2 * BLOCK, BLOCK), 0)
        - lax.broadcasted_iota(jnp.int32, (2 * BLOCK, BLOCK), 1)
        - (LANES + b)
    )
    value = jnp.where(d == 0, 1.0, 0.0).astype(BF16)
    slope = jnp.where(d == 1, 1.0, jnp.where(d == -1, -1.0, 0.0)).astype(BF16)
    return value, slope


def moved(ext, col, w):
    return jnp.dot(ext[:, col : col + 2 * BLOCK], w, preferred_element_type=F32)


def put(scratch, slot, x):
    for h in range(x.shape[1] // LANES):
        scratch[slot + h, :, :] = x[:, h * LANES : (h + 1) * LANES]


def start(copies, sem, first=0):
    started = [pltpu.make_async_copy(src, dst, sem.at[first + k]) for k, (src, dst) in enumerate(copies)]
    for copy in started:
        copy.start()
    return started


def load(copies, sem):
    for copy in start(copies, sem):
        copy.wait()


def fold(x):
    return x.reshape(-1, 8, LANES).sum(axis=0)


def block_sums(scratch, slot, a, current, store, accs):
    band = scratch.shape[1] - 2 * EDGE
    for r0 in range(0, band, ROWS_CHUNK):
        start = r0 + (EDGE - 1) + a
        for h in range(2):
            up = scratch[slot + h, pl.ds(start, ROWS_CHUNK), :]
            mid = scratch[slot + h, pl.ds(start + 1, ROWS_CHUNK), :]
            down = scratch[slot + h, pl.ds(start + 2, ROWS_CHUNK), :]
            gx = scratch[slot + 2 + h, pl.ds(start + 1, ROWS_CHUNK), :]
            gy = down - up
            e = current(r0, h * LANES) - mid
            if store is not None:
                store(r0, h * LANES, e.astype(BF16))
            accs = tuple(
                acc + fold(p) for acc, p in zip(accs, (gy * gy, gy * gx, gx * gx, gy * e, gx * e))
            )
    return accs


def place_sums(vec, accs, i, j):
    lane = lax.broadcasted_iota(jnp.int32, (1, LANES), 1)
    for q, acc in enumerate(accs):
        total = jnp.sum(jnp.sum(acc, axis=0, keepdims=True), axis=1, keepdims=True)
        total = total * (0.25 if q < 3 else 0.5)
        vec = jnp.where(lane == q * 8 + i * PGX + j, total, vec)
    return vec


def zeros():
    return tuple(jnp.zeros((8, LANES), F32) for _ in range(5))


def half_sums(ext, scratch, peaks, i, first_patch, current, store, vec):
    matrices = [shift_matrices(b) for _, b in peaks]
    blocks = [(j, m) for j in range(HALF) for m in range(PATCH // BLOCK)]

    def prepare(n):
        j, m = blocks[n]
        value, slope = matrices[j]
        col = j * PATCH + m * BLOCK
        put(scratch, 4 * (n % 2), moved(ext, col, value))
        put(scratch, 4 * (n % 2) + 2, moved(ext, col, slope))

    prepare(0)
    accs = zeros()
    for n, (j, m) in enumerate(blocks):
        if n + 1 < len(blocks):
            prepare(n + 1)
        a = peaks[j][0]
        col = j * PATCH + m * BLOCK
        accs = block_sums(
            scratch,
            4 * (n % 2),
            a,
            lambda r0, c, col=col: current(r0, col + c),
            None if store is None else (lambda r0, c, e, col=col: store(r0, col + c, e)),
            accs,
        )
        if m + 1 == PATCH // BLOCK:
            vec = place_sums(vec, accs, i, first_patch + j)
            accs = zeros()
    return vec


def pack_bands(peaks_ref, own_ref, following_ref, rim_ref, *refs):
    *middles, tile, sem = refs
    band = own_ref.shape[1]
    first = rim_ref.shape[1]
    cols = pl.ds(0, first)
    copies = [
        (own_ref.at[0, :, pl.ds(SPLIT, following_ref.shape[1])], following_ref.at[pl.ds(0, band)]),
        (own_ref.at[0, pl.ds(0, EDGE), cols], rim_ref.at[pl.ds(0, EDGE)]),
        (own_ref.at[0, pl.ds(band - EDGE, EDGE), cols], rim_ref.at[pl.ds(EDGE, EDGE)]),
    ]
    row = EDGE
    for ref in middles:
        copies.append((own_ref.at[0, pl.ds(row, ref.shape[0]), cols], ref))
        row += ref.shape[0]
    copies = start(copies, sem)
    lane = lax.broadcasted_iota(jnp.int32, tile.shape, 1)
    values = jnp.zeros(tile.shape, F32)
    for k in range(2 * PGY * PGX):
        values = jnp.where(lane == k, peaks_ref[k].astype(F32), values)
    tile[...] = values.astype(BF16)
    copies += start([(tile, following_ref.at[pl.ds(band, EXTRA), pl.ds(0, LANES)])], sem, len(copies))
    for copy in copies:
        copy.wait()


def pack_edges(own_ref, rim_ref, upward_ref, downward_ref, sem):
    band, width = own_ref.shape[1:]
    margin = width - (SPLIT - LANES)
    own, rim = pl.ds(0, margin), pl.ds(margin, rim_ref.shape[1])
    cols = pl.ds(SPLIT - LANES, margin)
    load(
        [
            (own_ref.at[0, pl.ds(0, EDGE), cols], upward_ref.at[:, own]),
            (own_ref.at[0, pl.ds(band - EDGE, EDGE), cols], downward_ref.at[:, own]),
            (rim_ref.at[pl.ds(0, EDGE)], upward_ref.at[:, rim]),
            (rim_ref.at[pl.ds(EDGE, EDGE)], downward_ref.at[:, rim]),
        ],
        sem,
    )


def pack_tail(own_ref, above_ref, below_ref, *refs):
    *tails, sem = refs
    band, full = own_ref.shape[1:]
    width = tails[0].shape[1]
    cols = pl.ds(full - width, width)
    edge = pl.ds(full - width - (SPLIT - LANES), width)
    areas = (
        (above_ref.at[:, edge], 0, EDGE),
        (own_ref.at[0, :, cols], EDGE, EDGE + band),
        (below_ref.at[:, edge], EDGE + band, 2 * EDGE + band),
    )
    copies, row = [], 0
    for ref in tails:
        end = row + ref.shape[0]
        for area, low, high in areas:
            lo, hi = max(row, low), min(end, high)
            if lo < hi:
                copies.append((area.at[pl.ds(lo - low, hi - lo)], ref.at[pl.ds(lo - row, hi - lo)]))
        row = end
    load(copies, sem)


def stacked(refs, cols, ext, row, into):
    copies = []
    for ref in refs:
        rows = ref.shape[0]
        copies.append((ref.at[:, cols], ext.at[pl.ds(row, rows), into]))
        row += rows
    return copies


def sums_kernel(
    where_ref, peaks_ref, own_ref, above_ref, below_ref, following_ref, rim_ref, *refs
):
    i = where_ref[0]
    band, width = own_ref.shape[1:]
    middles = refs[: len(MIDDLES)]
    res_ref, vec_ref, behind, ahead, following, current, scratch, sem = refs[len(MIDDLES) :]
    first = rim_ref.shape[1]
    left = SPLIT - LANES
    margin = width - left
    cols = pl.ds(0, margin)
    early = start(
        [
            (above_ref.at[:, cols], behind.at[pl.ds(0, EDGE), cols]),
            (own_ref.at[0, :, pl.ds(left, margin)], behind.at[pl.ds(EDGE, band), cols]),
            (below_ref.at[:, cols], behind.at[pl.ds(EDGE + band, EDGE), cols]),
            (following_ref, following),
        ],
        sem,
    )
    cols, edge = pl.ds(LANES, first), pl.ds(margin, first)
    late = start(
        [
            (above_ref.at[:, edge], ahead.at[pl.ds(0, EDGE), cols]),
            (rim_ref.at[pl.ds(0, EDGE)], ahead.at[pl.ds(EDGE, EDGE), cols]),
            *stacked(middles, pl.ds(0, first), ahead, 2 * EDGE, cols),
            (rim_ref.at[pl.ds(EDGE, EDGE)], ahead.at[pl.ds(EDGE + band - EDGE, EDGE), cols]),
            (below_ref.at[:, edge], ahead.at[pl.ds(EDGE + band, EDGE), cols]),
            (own_ref.at[0, :, pl.ds(0, SPLIT)], current),
        ],
        sem,
        len(early),
    )
    blank = jnp.zeros((band + 2 * EDGE, LANES), BF16)
    behind[:, margin:] = blank
    ahead[:, :LANES] = blank

    def source(ref):
        return lambda r0, c: ref[r0 : r0 + ROWS_CHUNK, c : c + LANES].astype(F32)

    def store(r0, c, e):
        res_ref[0, r0 : r0 + ROWS_CHUNK, c : c + LANES] = e

    vec = jnp.zeros((1, LANES), F32)
    for copy in early:
        copy.wait()
    sent = following[band : band + EXTRA, :LANES].astype(F32)
    place = lax.broadcasted_iota(jnp.int32, sent.shape, 1)
    spot = lax.broadcasted_iota(jnp.int32, sent.shape, 0)

    def next_peak(k, j):
        mine = jnp.logical_and(spot == 0, place == k * PGY * PGX + i * PGX + HALF + j)
        return jnp.sum(jnp.where(mine, sent, 0.0)).astype(jnp.int32)

    next_peaks = [[next_peak(k, j) for k in range(2)] for j in range(HALF)]
    vec = half_sums(behind, scratch, next_peaks, i, HALF, source(following), None, vec)
    for copy in late:
        copy.wait()
    own_peaks = [[peaks_ref[k * PGY * PGX + i * PGX + j] for k in range(2)] for j in range(HALF)]
    vec = half_sums(ahead, scratch, own_peaks, i, 0, source(current), store, vec)
    lane = lax.broadcasted_iota(jnp.int32, (1, LANES), 1)
    for k in range(2 * PGY * PGX):
        share = jnp.where(where_ref[1] == 0, peaks_ref[k], 0).astype(F32)
        vec = jnp.where(lane == 40 + k, share, vec)
    vec_ref[...] = jnp.broadcast_to(vec[None], vec_ref.shape)


def rest_kernel(
    where_ref, peaks_ref, rim_ref, above_ref, below_ref, *refs
):
    middles, refs = refs[: len(MIDDLES)], refs[len(MIDDLES) :]
    tails, refs = refs[: len(TAILS)], refs[len(TAILS) :]
    own_ref, _, res_ref, ext, scratch, sem = refs
    i = where_ref[0]
    known = rim_ref.shape[1]
    width = tails[0].shape[1]
    band = res_ref.shape[1]
    shared = known - (SPLIT - LANES)
    old, new = pl.ds(known - shared, shared), pl.ds(shared, width)
    edge = pl.ds(above_ref.shape[1] - shared, shared)
    cols = pl.ds(0, shared)
    load(
        [
            (above_ref.at[:, edge], ext.at[pl.ds(0, EDGE), cols]),
            (rim_ref.at[pl.ds(0, EDGE), old], ext.at[pl.ds(EDGE, EDGE), cols]),
            *stacked(middles, old, ext, 2 * EDGE, cols),
            (rim_ref.at[pl.ds(EDGE, EDGE), old], ext.at[pl.ds(band, EDGE), cols]),
            (below_ref.at[:, edge], ext.at[pl.ds(EDGE + band, EDGE), cols]),
            *stacked(tails, pl.ds(0, width), ext, 0, new),
        ],
        sem,
    )
    ext[:, shared + width :] = jnp.zeros((ext.shape[0], LANES), BF16)
    for j in range(HALF):
        a = peaks_ref[i * PGX + HALF + j]
        b = peaks_ref[PGY * PGX + i * PGX + HALF + j]
        value, _ = shift_matrices(b)
        for m in range(PATCH // BLOCK):
            col = j * PATCH + m * BLOCK
            slot = 2 * (m % 2)
            put(scratch, slot, moved(ext, col, value))
            for h in range(2):
                c = col + h * LANES
                mid = scratch[slot + h, pl.ds(EDGE + a, band), :]
                e = own_ref[0, :, c : c + LANES].astype(F32) - mid
                res_ref[0, :, c : c + LANES] = e.astype(BF16)


def tail_kernel(where_ref, sums_ref, field_ref, offsets_ref, rows_ref, wide_ref):
    sections = sums_ref.shape[0]
    band, width = field_ref.shape[2], field_ref.shape[3]
    nodes = PGY * PGX

    @pl.when(pl.program_id(0) == 0)
    def _():
        here = where_ref[2]
        lane = lax.broadcasted_iota(jnp.int32, (sections, LANES), 1)
        row = lax.broadcasted_iota(jnp.int32, (sections, LANES), 0)
        got = sums_ref[...]
        moved = jnp.where(row == 0, 0.0, pltpu.roll(got, 1, 0))
        behind = jnp.logical_and(lane < 40, lax.rem(lane, PGX) >= HALF)
        got = jnp.where(behind, moved, got)

        def part(k):
            return got if k == 0 else pltpu.roll(got, LANES - 8 * k, 1)

        valid = lane < nodes
        damping = LAMBDA * PATCH * PATCH
        first = part(0) + damping
        cross = part(1)
        second = part(2) + damping
        pull_y, pull_x = part(3), part(4)
        determinant = jnp.where(valid, first * second - cross * cross, 1.0)
        step_y = (second * pull_y - cross * pull_x) / determinant
        step_x = (first * pull_x - cross * pull_y) / determinant
        off_y = jnp.where(valid, part(5) + step_y, 0.0)
        off_x = jnp.where(valid, part(6) + step_x, 0.0)
        full_height = PGY * PATCH
        full_width = PGX * PATCH
        table = fit_table(PGY, PGX, PATCH, full_height, full_width)
        slot = lax.broadcasted_iota(jnp.int32, (1, LANES), 1)
        weights = []
        for m in range(2):
            w = jnp.zeros((1, LANES), F32)
            for p in range(nodes):
                w = jnp.where(slot == p, float(np.float32(table[m, p])), w)
            weights.append(w)
        scale = (full_height, full_width)
        for k, off in enumerate((off_y, off_x)):
            for m in range(2):
                coef = jnp.sum(off * weights[m], axis=1, keepdims=True)
                value = coef / scale[m] + (1.0 if k == m else 0.0)
                rows_ref[2 * k + m, :, :] = jnp.broadcast_to(value, (sections, LANES))
            rows_ref[4 + k, :, :] = off
        for k in range(2):
            mine = rows_ref[4 + k, pl.ds(here, 1), :]
            for i in range(PGY):
                offsets_ref[0, k, i : i + 1, :] = mine[:, i * PGX : (i + 1) * PGX]

        def advance(s, carry):
            uy, ux = carry
            l = [rows_ref[k, pl.ds(s, 1), :] for k in range(6)]
            return (l[0] * uy + l[1] * ux + l[4], l[2] * uy + l[3] * ux + l[5])

        zero = jnp.zeros((1, LANES), F32)
        u = lax.fori_loop(0, here + 1, advance, (zero, zero))
        pos = lax.broadcasted_iota(jnp.int32, (1, width), 1).astype(F32)
        pos = jnp.clip((pos + 0.5) / PATCH - 0.5, 0.0, PGX - 1.0)
        hats = [jnp.maximum(0.0, 1.0 - jnp.abs(pos - j)) for j in range(PGX)]
        for k in range(2):
            for i in range(PGY):
                wide = None
                for j in range(PGX):
                    node = jnp.sum(jnp.where(slot == i * PGX + j, u[k], 0.0), axis=1, keepdims=True)
                    term = node * hats[j]
                    wide = term if wide is None else wide + term
                wide_ref[2 * k + i, :, :] = jnp.broadcast_to(wide, (8, width))

    start = where_ref[3] + pl.program_id(0) * band
    for g in range(band // 8):
        pos = (start + g * 8 + lax.broadcasted_iota(jnp.int32, (8, LANES), 0)).astype(F32)
        pos = jnp.clip((pos + 0.5) / PATCH - 0.5, 0.0, PGY - 1.0)
        near = [jnp.maximum(0.0, 1.0 - jnp.abs(pos - i)) for i in range(PGY)]
        for k in range(2):
            for c in range(0, width, LANES):
                cols = slice(c, c + LANES)
                field_ref[0, k, g * 8 : g * 8 + 8, cols] = (
                    near[0] * wide_ref[2 * k, :, cols] + near[1] * wide_ref[2 * k + 1, :, cols]
                )


def vmem(shape=None, index=None):
    if shape is None:
        return pl.BlockSpec(memory_space=pltpu.VMEM)
    return pl.BlockSpec(shape, index)


SMEM = pl.BlockSpec(memory_space=pltpu.SMEM)


def params(mib):
    return pltpu.CompilerParams(vmem_limit_bytes=mib << 20)


def cost(flops, nbytes):
    return pl.CostEstimate(flops=flops, bytes_accessed=nbytes, transcendentals=0)


def per_device(sections, peaks):
    _, band, width = sections.shape
    place = lax.axis_index("rows")
    here = lax.axis_index("gz")
    where = jnp.stack([place * band // PATCH, place, here, place * band]).astype(jnp.int32)
    first = SPLIT + LANES
    peaks_own = peaks.reshape(-1)

    outer = band + 2 * EDGE
    margin = width - (SPLIT - LANES)
    anywhere = pl.BlockSpec(memory_space=pl.ANY)

    def packed(kernel, shapes, count, name, *operands):
        return pl.pallas_call(
            kernel,
            out_shape=tuple(jax.ShapeDtypeStruct(shape, BF16) for shape in shapes),
            in_specs=[anywhere] * len(operands),
            out_specs=tuple(anywhere for _ in shapes),
            scratch_shapes=[pltpu.SemaphoreType.DMA((count,))],
            compiler_params=params(4),
            cost_estimate=cost(0, sum(4 * r * c for r, c in shapes)),
            name=name,
        )(*operands)

    shapes = [(band + EXTRA, width - SPLIT), (2 * EDGE, first), *[(rows, first) for rows in MIDDLES]]
    following, rim, *middles = pl.pallas_call(
        pack_bands,
        out_shape=tuple(jax.ShapeDtypeStruct(shape, BF16) for shape in shapes),
        in_specs=[SMEM, pl.BlockSpec(memory_space=pltpu.HBM)],
        out_specs=tuple(anywhere for _ in shapes),
        scratch_shapes=[pltpu.VMEM((EXTRA, LANES), BF16), pltpu.SemaphoreType.DMA((4 + len(MIDDLES),))],
        compiler_params=params(4),
        cost_estimate=cost(0, 8 << 20),
        name="bands",
    )(peaks_own, sections)
    following = shift(following, "gz", -1)
    rim = shift(rim, "gz", 1)
    middles = [shift(x, "gz", 1) for x in middles]
    upward, downward = packed(pack_edges, ((EDGE, margin + first),) * 2, 4, "edges", sections, rim)
    above = shift(downward, "rows", 1)
    below = shift(upward, "rows", -1)
    shapes = tuple((rows, width - first) for rows in TAILS)
    tails = packed(pack_tail, shapes, 2 + len(TAILS), "tail", sections, above, below)
    tails = [shift(x, "gz", 1) for x in tails]

    extended = pltpu.VMEM((outer, first + LANES), BF16)
    scratch = pltpu.VMEM((8, outer, LANES), F32)
    half = (1, band, SPLIT)
    residual, sums = pl.pallas_call(
        sums_kernel,
        grid=(1,),
        out_shape=(
            jax.ShapeDtypeStruct((1, band, width), BF16),
            jax.ShapeDtypeStruct((lax.axis_size("rows"), 1, LANES), F32),
        ),
        in_specs=[SMEM, SMEM, *[anywhere] * (5 + len(MIDDLES))],
        out_specs=(vmem(half, lambda g: (0, 0, 0)), vmem()),
        scratch_shapes=[
            extended,
            extended,
            pltpu.VMEM((band + EXTRA, width - SPLIT), BF16),
            pltpu.VMEM((band, SPLIT), BF16),
            scratch,
            pltpu.SemaphoreType.DMA((9 + len(MIDDLES),)),
        ],
        compiler_params=params(24),
        cost_estimate=cost(10_000_000, 8 << 20),
        name="sums",
    )(where, peaks_own, sections, above, below, following, rim, *middles)

    sums = lax.all_to_all(sums, "rows", split_axis=0, concat_axis=0, tiled=True).sum(axis=0)
    everyone = jnp.broadcast_to(sums[None], (lax.axis_size("gz"), 1, LANES))
    residual, _ = lax.optimization_barrier((residual, sums))
    everyone = lax.all_to_all(everyone, "gz", split_axis=0, concat_axis=0, tiled=True)
    everyone = everyone.reshape(-1, LANES)

    residual = pl.pallas_call(
        rest_kernel,
        grid=(1,),
        out_shape=jax.ShapeDtypeStruct((1, band, width), BF16),
        in_specs=[SMEM, SMEM, *[anywhere] * (3 + len(MIDDLES + TAILS)), vmem(half, lambda g: (0, 0, 1)), anywhere],
        out_specs=vmem(half, lambda g: (0, 0, 1)),
        scratch_shapes=[
            extended,
            pltpu.VMEM((4, outer, LANES), F32),
            pltpu.SemaphoreType.DMA((4 + len(MIDDLES + TAILS),)),
        ],
        input_output_aliases={6 + len(MIDDLES + TAILS): 0},
        compiler_params=params(24),
        cost_estimate=cost(5_000_000, 4 << 20),
        name="rest",
    )(where, peaks_own, rim, above, below, *middles, *tails, sections, residual)

    everyone, residual = lax.optimization_barrier((everyone, residual))
    step = 32
    field, offsets = pl.pallas_call(
        tail_kernel,
        grid=(band // step,),
        out_shape=(
            jax.ShapeDtypeStruct((1, 2, band, width), F32),
            jax.ShapeDtypeStruct((1, 2, PGY, PGX), F32),
        ),
        in_specs=[SMEM, vmem()],
        out_specs=(vmem((1, 2, step, width), lambda g: (0, 0, g, 0)), vmem()),
        scratch_shapes=[
            pltpu.VMEM((6, everyone.shape[0], LANES), F32),
            pltpu.VMEM((4, 8, width), F32),
        ],
        compiler_params=params(24),
        cost_estimate=cost(10_000_000, 8 << 20),
        name="spread",
    )(where, everyone)
    return (field, offsets, residual)


def solution(mesh):
    placed = (P("gz", "rows", None), P("gz", None, None, None))
    return jax.shard_map(
        per_device,
        mesh=mesh,
        in_specs=placed,
        out_specs=(P("gz", None, "rows", None), P("gz", None, None, None), P("gz", "rows", None)),
        check_vma=False,
    )
```

```python
import jax
import jax.numpy as jnp
import numpy as np
from jax import lax
from jax.experimental import pallas as pl
from jax.experimental.pallas import tpu as pltpu
from jax.sharding import PartitionSpec as P

PATCH = 1024
LAMBDA = 0.002
RIDGE = 0.05

PGY = 2
PGX = 4
HALF = PGX // 2
SPLIT = HALF * PATCH
LANES = 128
BLOCK = 256
EDGE = 32
EXTRA = 16
MIDDLES = (192,)
TAILS = (128, 128)
ROWS_CHUNK = 32
F32 = jnp.float32
BF16 = jnp.bfloat16


def shift(value, axis, steps):
    count = lax.axis_size(axis)
    first, last = (max(0, -steps), min(count, count - steps))
    return lax.ppermute(value, axis, [(source, source + steps) for source in range(first, last)])


def invert_three(matrix):
    a, b, c = (matrix[0, 0], matrix[0, 1], matrix[0, 2])
    d, e, f = (matrix[1, 0], matrix[1, 1], matrix[1, 2])
    g, h, k = (matrix[2, 0], matrix[2, 1], matrix[2, 2])
    cof = np.array(
        [
            [e * k - f * h, c * h - b * k, b * f - c * e],
            [f * g - d * k, a * k - c * g, c * d - a * f],
            [d * h - e * g, b * g - a * h, a * e - b * d],
        ]
    )
    return cof / (a * (e * k - f * h) - b * (d * k - f * g) + c * (d * h - e * g))


def fit_table(pgy, pgx, patch, height, width):
    yy = ((np.arange(pgy) + 0.5) * patch - height / 2.0) / height
    xx = ((np.arange(pgx) + 0.5) * patch - width / 2.0) / width
    design = np.stack([np.repeat(yy, pgx), np.tile(xx, pgy), np.ones(pgy * pgx)], 1)
    ridge_matrix = np.array([[RIDGE, 0.0, 0.0], [0.0, RIDGE, 0.0], [0.0, 0.0, 0.0]])
    gram = design.T @ design + ridge_matrix
    return invert_three(gram) @ design.T


def shift_matrices(b):
    d = (
        lax.broadcasted_iota(jnp.int32, (2 * BLOCK, BLOCK), 0)
        - lax.broadcasted_iota(jnp.int32, (2 * BLOCK, BLOCK), 1)
        - (LANES + b)
    )
    value = jnp.where(d == 0, 1.0, 0.0).astype(BF16)
    slope = jnp.where(d == 1, 1.0, jnp.where(d == -1, -1.0, 0.0)).astype(BF16)
    return value, slope


def moved(ext, col, w):
    return jnp.dot(ext[:, col : col + 2 * BLOCK], w, preferred_element_type=F32)


def put(scratch, slot, x):
    for h in range(x.shape[1] // LANES):
        scratch[slot + h, :, :] = x[:, h * LANES : (h + 1) * LANES]


def start(copies, sem, first=0):
    started = [pltpu.make_async_copy(src, dst, sem.at[first + k]) for k, (src, dst) in enumerate(copies)]
    for copy in started:
        copy.start()
    return started


def load(copies, sem):
    for copy in start(copies, sem):
        copy.wait()


def fold(x):
    return x.reshape(-1, 8, LANES).sum(axis=0)


def block_sums(scratch, slot, a, current, store, accs):
    band = scratch.shape[1] - 2 * EDGE
    for r0 in range(0, band, ROWS_CHUNK):
        start = r0 + (EDGE - 1) + a
        for h in range(2):
            up = scratch[slot + h, pl.ds(start, ROWS_CHUNK), :]
            mid = scratch[slot + h, pl.ds(start + 1, ROWS_CHUNK), :]
            down = scratch[slot + h, pl.ds(start + 2, ROWS_CHUNK), :]
            gx = scratch[slot + 2 + h, pl.ds(start + 1, ROWS_CHUNK), :]
            gy = down - up
            e = current(r0, h * LANES) - mid
            if store is not None:
                store(r0, h * LANES, e.astype(BF16))
            accs = tuple(
                acc + fold(p) for acc, p in zip(accs, (gy * gy, gy * gx, gx * gx, gy * e, gx * e))
            )
    return accs


def place_sums(vec, accs, i, j):
    lane = lax.broadcasted_iota(jnp.int32, (1, LANES), 1)
    for q, acc in enumerate(accs):
        total = jnp.sum(jnp.sum(acc, axis=0, keepdims=True), axis=1, keepdims=True)
        total = total * (0.25 if q < 3 else 0.5)
        vec = jnp.where(lane == q * 8 + i * PGX + j, total, vec)
    return vec


def peak(peaks_ref, k):
    return peaks_ref[0, k // (PGY * PGX), k // PGX % PGY, k % PGX]


def zeros():
    return tuple(jnp.zeros((8, LANES), F32) for _ in range(5))


def half_sums(ext, scratch, peaks, i, first_patch, current, store, vec):
    matrices = [shift_matrices(b) for _, b in peaks]
    blocks = [(j, m) for j in range(HALF) for m in range(PATCH // BLOCK)]

    def prepare(n):
        j, m = blocks[n]
        value, slope = matrices[j]
        col = j * PATCH + m * BLOCK
        put(scratch, 4 * (n % 2), moved(ext, col, value))
        put(scratch, 4 * (n % 2) + 2, moved(ext, col, slope))

    prepare(0)
    accs = zeros()
    for n, (j, m) in enumerate(blocks):
        if n + 1 < len(blocks):
            prepare(n + 1)
        a = peaks[j][0]
        col = j * PATCH + m * BLOCK
        accs = block_sums(
            scratch,
            4 * (n % 2),
            a,
            lambda r0, c, col=col: current(r0, col + c),
            None if store is None else (lambda r0, c, e, col=col: store(r0, col + c, e)),
            accs,
        )
        if m + 1 == PATCH // BLOCK:
            vec = place_sums(vec, accs, i, first_patch + j)
            accs = zeros()
    return vec


def pack_bands(peaks_ref, own_ref, following_ref, rim_ref, *refs):
    *parts, tile, sem = refs
    middles, tails = parts[: len(MIDDLES)], parts[len(MIDDLES) :]
    band = own_ref.shape[1]
    first = rim_ref.shape[1]
    cols = pl.ds(0, first)
    copies = [
        (own_ref.at[0, :, pl.ds(SPLIT, following_ref.shape[1])], following_ref.at[pl.ds(0, band)]),
        (own_ref.at[0, pl.ds(0, EDGE), cols], rim_ref.at[pl.ds(0, EDGE)]),
        (own_ref.at[0, pl.ds(band - EDGE, EDGE), cols], rim_ref.at[pl.ds(EDGE, EDGE)]),
    ]
    row = EDGE
    for ref in middles:
        copies.append((own_ref.at[0, pl.ds(row, ref.shape[0]), cols], ref))
        row += ref.shape[0]
    row = 0
    for ref in tails:
        copies.append((own_ref.at[0, pl.ds(row, ref.shape[0]), pl.ds(first, ref.shape[1])], ref))
        row += ref.shape[0]
    copies = start(copies, sem)
    lane = lax.broadcasted_iota(jnp.int32, tile.shape, 1)
    values = jnp.zeros(tile.shape, F32)
    for k in range(2 * PGY * PGX):
        values = jnp.where(lane == k, peak(peaks_ref, k).astype(F32), values)
    tile[...] = values.astype(BF16)
    copies += start([(tile, following_ref.at[pl.ds(band, EXTRA), pl.ds(0, LANES)])], sem, len(copies))
    for copy in copies:
        copy.wait()


def pack_edges(own_ref, rim_ref, upward_ref, downward_ref, sem):
    band, width = own_ref.shape[1:]
    margin = width - (SPLIT - LANES)
    own, rim = pl.ds(0, margin), pl.ds(margin, rim_ref.shape[1])
    cols = pl.ds(SPLIT - LANES, margin)
    load(
        [
            (own_ref.at[0, pl.ds(0, EDGE), cols], upward_ref.at[:, own]),
            (own_ref.at[0, pl.ds(band - EDGE, EDGE), cols], downward_ref.at[:, own]),
            (rim_ref.at[pl.ds(0, EDGE)], upward_ref.at[:, rim]),
            (rim_ref.at[pl.ds(EDGE, EDGE)], downward_ref.at[:, rim]),
        ],
        sem,
    )


def pack_tail(above_ref, below_ref, edge_ref, sem):
    width = edge_ref.shape[1]
    edge = pl.ds(LANES + HALF * PATCH - width, width)
    load(
        [
            (above_ref.at[:, edge], edge_ref.at[pl.ds(0, EDGE)]),
            (below_ref.at[:, edge], edge_ref.at[pl.ds(EDGE, EDGE)]),
        ],
        sem,
    )


def stacked(refs, cols, ext, row, into):
    copies = []
    for ref in refs:
        rows = ref.shape[0]
        copies.append((ref.at[:, cols], ext.at[pl.ds(row, rows), into]))
        row += rows
    return copies


def sums_kernel(
    where_ref, peaks_ref, own_ref, above_ref, below_ref, following_ref, rim_ref, *refs
):
    i = where_ref[0]
    band, width = own_ref.shape[1:]
    middles = refs[: len(MIDDLES)]
    res_ref, vec_ref, behind, ahead, following, current, scratch, sem = refs[len(MIDDLES) :]
    first = rim_ref.shape[1]
    left = SPLIT - LANES
    margin = width - left
    cols = pl.ds(0, margin)
    early = start(
        [
            (above_ref.at[:, cols], behind.at[pl.ds(0, EDGE), cols]),
            (own_ref.at[0, :, pl.ds(left, margin)], behind.at[pl.ds(EDGE, band), cols]),
            (below_ref.at[:, cols], behind.at[pl.ds(EDGE + band, EDGE), cols]),
            (following_ref, following),
        ],
        sem,
    )
    cols, edge = pl.ds(LANES, first), pl.ds(margin, first)
    late = start(
        [
            (above_ref.at[:, edge], ahead.at[pl.ds(0, EDGE), cols]),
            (rim_ref.at[pl.ds(0, EDGE)], ahead.at[pl.ds(EDGE, EDGE), cols]),
            *stacked(middles, pl.ds(0, first), ahead, 2 * EDGE, cols),
            (rim_ref.at[pl.ds(EDGE, EDGE)], ahead.at[pl.ds(EDGE + band - EDGE, EDGE), cols]),
            (below_ref.at[:, edge], ahead.at[pl.ds(EDGE + band, EDGE), cols]),
            (own_ref.at[0, :, pl.ds(0, SPLIT)], current),
        ],
        sem,
        len(early),
    )
    blank = jnp.zeros((band + 2 * EDGE, LANES), BF16)
    behind[:, margin:] = blank
    ahead[:, :LANES] = blank

    def source(ref):
        return lambda r0, c: ref[r0 : r0 + ROWS_CHUNK, c : c + LANES].astype(F32)

    def store(r0, c, e):
        res_ref[0, r0 : r0 + ROWS_CHUNK, c : c + LANES] = e

    vec = jnp.zeros((1, LANES), F32)
    for copy in early:
        copy.wait()
    sent = following[band : band + EXTRA, :LANES].astype(F32)
    place = lax.broadcasted_iota(jnp.int32, sent.shape, 1)
    spot = lax.broadcasted_iota(jnp.int32, sent.shape, 0)

    def next_peak(k, j):
        mine = jnp.logical_and(spot == 0, place == k * PGY * PGX + i * PGX + HALF + j)
        return jnp.sum(jnp.where(mine, sent, 0.0)).astype(jnp.int32)

    next_peaks = [[next_peak(k, j) for k in range(2)] for j in range(HALF)]
    vec = half_sums(behind, scratch, next_peaks, i, HALF, source(following), None, vec)
    for copy in late:
        copy.wait()
    own_peaks = [[peaks_ref[0, k, i, j] for k in range(2)] for j in range(HALF)]
    vec = half_sums(ahead, scratch, own_peaks, i, 0, source(current), store, vec)
    lane = lax.broadcasted_iota(jnp.int32, (1, LANES), 1)
    for k in range(2 * PGY * PGX):
        share = jnp.where(where_ref[1] == 0, peak(peaks_ref, k), 0).astype(F32)
        vec = jnp.where(lane == 40 + k, share, vec)
    vec_ref[...] = jnp.broadcast_to(vec[None], vec_ref.shape)


def rest_kernel(
    where_ref, peaks_ref, rim_ref, above_ref, below_ref, *refs
):
    middles, refs = refs[: len(MIDDLES)], refs[len(MIDDLES) :]
    tails, refs = refs[: len(TAILS)], refs[len(TAILS) :]
    tail_edge_ref, own_ref, _, res_ref, ext, scratch, current, sem = refs
    i = where_ref[0]
    known = rim_ref.shape[1]
    width = tails[0].shape[1]
    band = res_ref.shape[1]
    shared = known - (SPLIT - LANES)
    old, new = pl.ds(known - shared, shared), pl.ds(shared, width)
    edge = pl.ds(above_ref.shape[1] - shared, shared)
    cols = pl.ds(0, shared)
    load(
        [
            (above_ref.at[:, edge], ext.at[pl.ds(0, EDGE), cols]),
            (rim_ref.at[pl.ds(0, EDGE), old], ext.at[pl.ds(EDGE, EDGE), cols]),
            *stacked(middles, old, ext, 2 * EDGE, cols),
            (rim_ref.at[pl.ds(EDGE, EDGE), old], ext.at[pl.ds(band, EDGE), cols]),
            (below_ref.at[:, edge], ext.at[pl.ds(EDGE + band, EDGE), cols]),
            (tail_edge_ref.at[pl.ds(0, EDGE)], ext.at[pl.ds(0, EDGE), new]),
            *stacked(tails, pl.ds(0, width), ext, EDGE, new),
            (tail_edge_ref.at[pl.ds(EDGE, EDGE)], ext.at[pl.ds(EDGE + band, EDGE), new]),
            (own_ref.at[0, :, pl.ds(SPLIT, own_ref.shape[2] - SPLIT)], current),
        ],
        sem,
    )
    ext[:, shared + width :] = jnp.zeros((ext.shape[0], LANES), BF16)
    for j in range(HALF):
        a = peaks_ref[0, 0, i, HALF + j]
        b = peaks_ref[0, 1, i, HALF + j]
        value, _ = shift_matrices(b)
        for m in range(PATCH // BLOCK):
            col = j * PATCH + m * BLOCK
            slot = 2 * (m % 2)
            put(scratch, slot, moved(ext, col, value))
            for h in range(2):
                c = col + h * LANES
                mid = scratch[slot + h, pl.ds(EDGE + a, band), :]
                e = current[:, c : c + LANES].astype(F32) - mid
                res_ref[0, :, c : c + LANES] = e.astype(BF16)


def tail_kernel(where_ref, sums_ref, field_ref, offsets_ref, rows_ref, wide_ref):
    sections = sums_ref.shape[0]
    band, width = field_ref.shape[2], field_ref.shape[3]
    nodes = PGY * PGX

    @pl.when(pl.program_id(0) == 0)
    def _():
        here = where_ref[2]
        lane = lax.broadcasted_iota(jnp.int32, (sections, LANES), 1)
        row = lax.broadcasted_iota(jnp.int32, (sections, LANES), 0)
        got = sums_ref[...]
        moved = jnp.where(row == 0, 0.0, pltpu.roll(got, 1, 0))
        behind = jnp.logical_and(lane < 40, lax.rem(lane, PGX) >= HALF)
        got = jnp.where(behind, moved, got)

        def part(k):
            return got if k == 0 else pltpu.roll(got, LANES - 8 * k, 1)

        valid = lane < nodes
        damping = LAMBDA * PATCH * PATCH
        first = part(0) + damping
        cross = part(1)
        second = part(2) + damping
        pull_y, pull_x = part(3), part(4)
        determinant = jnp.where(valid, first * second - cross * cross, 1.0)
        step_y = (second * pull_y - cross * pull_x) / determinant
        step_x = (first * pull_x - cross * pull_y) / determinant
        off_y = jnp.where(valid, part(5) + step_y, 0.0)
        off_x = jnp.where(valid, part(6) + step_x, 0.0)
        full_height = PGY * PATCH
        full_width = PGX * PATCH
        table = fit_table(PGY, PGX, PATCH, full_height, full_width)
        slot = lax.broadcasted_iota(jnp.int32, (1, LANES), 1)
        weights = []
        for m in range(2):
            w = jnp.zeros((1, LANES), F32)
            for p in range(nodes):
                w = jnp.where(slot == p, float(np.float32(table[m, p])), w)
            weights.append(w)
        scale = (full_height, full_width)
        for k, off in enumerate((off_y, off_x)):
            for m in range(2):
                coef = jnp.sum(off * weights[m], axis=1, keepdims=True)
                value = coef / scale[m] + (1.0 if k == m else 0.0)
                rows_ref[2 * k + m, :, :] = jnp.broadcast_to(value, (sections, LANES))
            rows_ref[4 + k, :, :] = off
        for k in range(2):
            mine = rows_ref[4 + k, pl.ds(here, 1), :]
            for i in range(PGY):
                offsets_ref[0, k, i : i + 1, :] = mine[:, i * PGX : (i + 1) * PGX]

        def advance(s, carry):
            uy, ux = carry
            l = [rows_ref[k, pl.ds(s, 1), :] for k in range(6)]
            return (l[0] * uy + l[1] * ux + l[4], l[2] * uy + l[3] * ux + l[5])

        zero = jnp.zeros((1, LANES), F32)
        u = lax.fori_loop(0, here + 1, advance, (zero, zero))
        pos = lax.broadcasted_iota(jnp.int32, (1, width), 1).astype(F32)
        pos = jnp.clip((pos + 0.5) / PATCH - 0.5, 0.0, PGX - 1.0)
        hats = [jnp.maximum(0.0, 1.0 - jnp.abs(pos - j)) for j in range(PGX)]
        for k in range(2):
            for i in range(PGY):
                wide = None
                for j in range(PGX):
                    node = jnp.sum(jnp.where(slot == i * PGX + j, u[k], 0.0), axis=1, keepdims=True)
                    term = node * hats[j]
                    wide = term if wide is None else wide + term
                wide_ref[2 * k + i, :, :] = jnp.broadcast_to(wide, (8, width))

    start = where_ref[3] + pl.program_id(0) * band
    for g in range(band // 8):
        pos = (start + g * 8 + lax.broadcasted_iota(jnp.int32, (8, LANES), 0)).astype(F32)
        pos = jnp.clip((pos + 0.5) / PATCH - 0.5, 0.0, PGY - 1.0)
        near = [jnp.maximum(0.0, 1.0 - jnp.abs(pos - i)) for i in range(PGY)]
        for k in range(2):
            for c in range(0, width, LANES):
                cols = slice(c, c + LANES)
                field_ref[0, k, g * 8 : g * 8 + 8, cols] = (
                    near[0] * wide_ref[2 * k, :, cols] + near[1] * wide_ref[2 * k + 1, :, cols]
                )


def vmem(shape=None, index=None):
    if shape is None:
        return pl.BlockSpec(memory_space=pltpu.VMEM)
    return pl.BlockSpec(shape, index)


SMEM = pl.BlockSpec(memory_space=pltpu.SMEM)


def params(mib):
    return pltpu.CompilerParams(vmem_limit_bytes=mib << 20)


def cost(flops, nbytes):
    return pl.CostEstimate(flops=flops, bytes_accessed=nbytes, transcendentals=0)


def per_device(sections, peaks):
    _, band, width = sections.shape
    place = lax.axis_index("rows")
    here = lax.axis_index("gz")
    where = jnp.stack([place * band // PATCH, place, here, place * band]).astype(jnp.int32)
    first = SPLIT + LANES

    outer = band + 2 * EDGE
    margin = width - (SPLIT - LANES)
    stored = pl.BlockSpec(memory_space=pltpu.HBM)

    def packed(kernel, shapes, count, name, *operands):
        return pl.pallas_call(
            kernel,
            out_shape=tuple(jax.ShapeDtypeStruct(shape, BF16) for shape in shapes),
            in_specs=[stored] * len(operands),
            out_specs=tuple(stored for _ in shapes),
            scratch_shapes=[pltpu.SemaphoreType.DMA((count,))],
            compiler_params=params(4),
            cost_estimate=cost(0, sum(4 * r * c for r, c in shapes)),
            name=name,
        )(*operands)

    shapes = [(band + EXTRA, width - SPLIT), (2 * EDGE, first), *[(rows, first) for rows in MIDDLES]]
    shapes += [(rows, width - first) for rows in TAILS]
    following, rim, *parts = pl.pallas_call(
        pack_bands,
        out_shape=tuple(jax.ShapeDtypeStruct(shape, BF16) for shape in shapes),
        in_specs=[SMEM, stored],
        out_specs=tuple(stored for _ in shapes),
        scratch_shapes=[pltpu.VMEM((EXTRA, LANES), BF16), pltpu.SemaphoreType.DMA((4 + len(MIDDLES + TAILS),))],
        compiler_params=params(4),
        cost_estimate=cost(0, 8 << 20),
        name="bands",
    )(peaks, sections)
    following = shift(following, "gz", -1)
    rim = shift(rim, "gz", 1)
    middles = [shift(x, "gz", 1) for x in parts[: len(MIDDLES)]]
    tails = [shift(x, "gz", 1) for x in parts[len(MIDDLES) :]]
    upward, downward = packed(pack_edges, ((EDGE, margin + first),) * 2, 4, "edges", sections, rim)
    above = shift(downward, "rows", 1)
    below = shift(upward, "rows", -1)
    (tail_edge,) = packed(pack_tail, ((2 * EDGE, width - first),), 2, "tail", above, below)
    tail_edge = shift(tail_edge, "gz", 1)

    extended = pltpu.VMEM((outer, first + LANES), BF16)
    scratch = pltpu.VMEM((8, outer, LANES), F32)
    half = (1, band, SPLIT)
    residual, sums = pl.pallas_call(
        sums_kernel,
        grid=(1,),
        out_shape=(
            jax.ShapeDtypeStruct((1, band, width), BF16),
            jax.ShapeDtypeStruct((lax.axis_size("rows"), 1, LANES), F32),
        ),
        in_specs=[SMEM, SMEM, *[stored] * (5 + len(MIDDLES))],
        out_specs=(vmem(half, lambda g: (0, 0, 0)), vmem()),
        scratch_shapes=[
            extended,
            extended,
            pltpu.VMEM((band + EXTRA, width - SPLIT), BF16),
            pltpu.VMEM((band, SPLIT), BF16),
            scratch,
            pltpu.SemaphoreType.DMA((9 + len(MIDDLES),)),
        ],
        compiler_params=params(24),
        cost_estimate=cost(10_000_000, 8 << 20),
        name="sums",
    )(where, peaks, sections, above, below, following, rim, *middles)

    sums = lax.all_to_all(sums, "rows", split_axis=0, concat_axis=0, tiled=True).sum(axis=0)
    everyone = jnp.broadcast_to(sums[None], (lax.axis_size("gz"), 1, LANES))
    residual, _ = lax.optimization_barrier((residual, sums))
    everyone = lax.all_to_all(everyone, "gz", split_axis=0, concat_axis=0, tiled=True)
    everyone = everyone.reshape(-1, LANES)

    residual = pl.pallas_call(
        rest_kernel,
        grid=(1,),
        out_shape=jax.ShapeDtypeStruct((1, band, width), BF16),
        in_specs=[SMEM, SMEM, *[stored] * (6 + len(MIDDLES + TAILS))],
        out_specs=vmem(half, lambda g: (0, 0, 1)),
        scratch_shapes=[
            extended,
            pltpu.VMEM((4, outer, LANES), F32),
            pltpu.VMEM((band, width - SPLIT), BF16),
            pltpu.SemaphoreType.DMA((7 + len(MIDDLES + TAILS),)),
        ],
        input_output_aliases={7 + len(MIDDLES + TAILS): 0},
        compiler_params=params(24),
        cost_estimate=cost(5_000_000, 4 << 20),
        name="rest",
    )(where, peaks, rim, above, below, *middles, *tails, tail_edge, sections, residual)

    everyone, residual = lax.optimization_barrier((everyone, residual))
    step = 32
    field, offsets = pl.pallas_call(
        tail_kernel,
        grid=(band // step,),
        out_shape=(
            jax.ShapeDtypeStruct((1, 2, band, width), F32),
            jax.ShapeDtypeStruct((1, 2, PGY, PGX), F32),
        ),
        in_specs=[SMEM, vmem()],
        out_specs=(vmem((1, 2, step, width), lambda g: (0, 0, g, 0)), vmem()),
        scratch_shapes=[
            pltpu.VMEM((6, everyone.shape[0], LANES), F32),
            pltpu.VMEM((4, 8, width), F32),
        ],
        compiler_params=params(24),
        cost_estimate=cost(10_000_000, 8 << 20),
        name="spread",
    )(where, everyone)
    return (field, offsets, residual)


def solution(mesh):
    placed = (P("gz", "rows", None), P("gz", None, None, None))
    return jax.shard_map(
        per_device,
        mesh=mesh,
        in_specs=placed,
        out_specs=(P("gz", None, "rows", None), P("gz", None, None, None), P("gz", "rows", None)),
        check_vma=False,
    )
```
